32 devices in a mesh: fsdp: 2 (over x), dp: 4 (over z), owner: 4 (over y, core).
Axes of the slice: x: 2, y: 2, z: 4, core: 2. Of those that a mesh axis runs over, the one named last changes fastest.
Arguments:
- hidden: bfloat16 [32, 256, 4096], P(('fsdp', 'dp', 'owner')), may hold values from -6 to 6
- norm_gain: float32 [4096], replicated, may hold values from 0.1 to 1.9
- query_weight: bfloat16 [4096, 2048], P(('fsdp', 'dp')), may hold values from -0.09375 to 0.09375
- key_value_weight: bfloat16 [4096, 1024], P(('fsdp', 'dp')), may hold values from -0.09375 to 0.09375
- lengths: int32 [32], P(('fsdp', 'dp', 'owner')), may hold values from 128 to 256, as said below
- cotangent: bfloat16 [32, 256, 2048], P(('fsdp', 'dp', 'owner')), may hold values from -6 to 6
- cartridge: float32 [512, 1024], P('owner'), may hold values from -48 to 48
- adam_first_moment: float32 [512, 1024], P('owner'), may hold values from -6 to 6
- adam_second_moment: float32 [512, 1024], P('owner'), may hold values from 0.01 to 1
Outputs:
- attention_out: bfloat16 [32, 256, 2048], P(('fsdp', 'dp', 'owner'))
- new_cartridge: float32 [512, 1024], P('owner')
- new_first: float32 [512, 1024], P('owner')
- new_second: float32 [512, 1024], P('owner')
The draws below stay inside these ranges and needn't reach their ends.
Inputs may be any that keep to these rules, and one draw needn't show every extreme that they name: `lengths`: each conversation's live tokens are its first rows; the rows after them are padding; some conversation is full.
All inputs are finite; a program needn't handle non-finite values.
Results may differ from the reference program's by a relative error of at most 0.008.
The reference program's roundings to bfloat16 on the way count: a program that leaves them out, or rounds other values in their place, can miss the bound.
Values may be sent and summed in bfloat16 or wider, within the bound.
A program may use at most 128 MiB of HBM per device.

```python
import math
import jax
import jax.numpy as jnp
from jax import lax

MODEL_WIDTH = 4096
HEAD_SIZE = 128
QUERY_HEADS = 16
KEY_VALUE_HEADS = 4
S = 256
STEP = 50
PREFIX_TOKENS = 512
CONVS = 32


def draw_lengths(key, part):
    counts = jax.random.randint(jax.random.fold_in(key, 11), (CONVS,), S // 2, S + 1, dtype=jnp.int32)
    full_index = jax.random.randint(jax.random.fold_in(key, 12), (), 0, CONVS, dtype=jnp.int32)
    short_index = (full_index + jax.random.randint(jax.random.fold_in(key, 13), (), 1, CONVS, dtype=jnp.int32)) % CONVS
    places = jnp.arange(CONVS, dtype=jnp.int32)
    counts = jnp.where(places == full_index, S, counts)
    counts = jnp.where(places == short_index, S // 2, counts)
    return counts.astype(jnp.int32)


def draw_cartridge(key, part):
    column_count = 2 * KEY_VALUE_HEADS * HEAD_SIZE
    return jnp.clip(2.0 * jax.random.normal(jax.random.fold_in(key, 24), (PREFIX_TOKENS, column_count), jnp.float32), -8.0, 8.0)


def level_of(own_key, shape, shards, low, high):
    def one(axis_at, shards_of):
        steps = jax.random.uniform(jax.random.fold_in(jax.random.fold_in(own_key, 6), axis_at), (shards_of,), jnp.float32, low / len(shards), high / len(shards))
        return jnp.repeat(jnp.exp(steps), shape[axis_at] // shards_of).reshape((-1,) + (1,) * (len(shape) - axis_at - 1))

    loudness = one(*shards[0])
    for cut in shards[1:]:
        loudness = loudness * one(*cut)
    return loudness


def bell_draw(key, dims, scale, reach, cuts=(), kind=jnp.bfloat16):
    drawn = jax.random.normal(key, dims, jnp.float32) * scale
    if len(cuts) > 0:
        drawn = level_of(key, dims, cuts, -0.22, 0.18) * drawn
    return jnp.clip(drawn, min=-reach, max=reach).astype(kind)


def setup_inputs(seed: int = 0) -> dict:
    arg_keys = jax.random.split(jax.random.key(seed), 10)
    hidden = bell_draw(arg_keys[0], (CONVS, S, MODEL_WIDTH), 1.0, 6.0, ((0, 32),))
    norm_gain = jnp.clip(1.0 + 0.18 * jax.random.normal(arg_keys[1], (MODEL_WIDTH,), jnp.float32), 0.1, 1.9)
    query_weight = bell_draw(arg_keys[2], (MODEL_WIDTH, QUERY_HEADS * HEAD_SIZE), MODEL_WIDTH ** -0.5, 0.09375, ((0, 8),))
    key_value_weight = bell_draw(arg_keys[3], (MODEL_WIDTH, 2 * KEY_VALUE_HEADS * HEAD_SIZE), MODEL_WIDTH ** -0.5, 0.09375, ((0, 8),))
    lengths = draw_lengths(jax.random.fold_in(arg_keys[9], 71), 0)
    cotangent = bell_draw(arg_keys[5], (CONVS, S, QUERY_HEADS * HEAD_SIZE), 1.0, 6.0, ((0, 32),))
    cartridge = draw_cartridge(jax.random.fold_in(arg_keys[9], 71), 0)
    adam_first_moment = bell_draw(arg_keys[7], (PREFIX_TOKENS, 2 * KEY_VALUE_HEADS * HEAD_SIZE), 1.0, 6.0, ((0, 4),), jnp.float32)
    adam_second_moment = jnp.clip(jnp.exp(math.log(1.0) - 4.6051702 * jax.random.uniform(arg_keys[8], (PREFIX_TOKENS, 2 * KEY_VALUE_HEADS * HEAD_SIZE), jnp.float32) ** level_of(arg_keys[8], (PREFIX_TOKENS, 2 * KEY_VALUE_HEADS * HEAD_SIZE), ((0, 4),), -0.2, 0.2)), 0.01, 1.0)
    return dict(hidden=hidden, norm_gain=norm_gain, query_weight=query_weight, key_value_weight=key_value_weight, lengths=lengths, cotangent=cotangent, cartridge=cartridge, adam_first_moment=adam_first_moment, adam_second_moment=adam_second_moment)


def rotary_heads(values, offset):
    sequence_rows = values.shape[0]
    half_size = values.shape[2] // 2
    exponent = jnp.arange(half_size, dtype=jnp.float32) * (2.0 / values.shape[2])
    inverse = jnp.power(jnp.float32(500000.0), -exponent)
    position = (offset + jnp.arange(sequence_rows)).astype(jnp.float32)
    angles = position[:, None] * inverse[None, :]
    cosine = jnp.cos(angles)[:, None, :]
    sine = jnp.sin(angles)[:, None, :]
    first_half = values[..., :half_size]
    second_half = values[..., half_size:]
    return jnp.concatenate([first_half * cosine - second_half * sine, second_half * cosine + first_half * sine], axis=-1)

def adam_update(current, moment_one, moment_two, prefix_gradient):
    one_new = 0.9 * moment_one + 0.1 * prefix_gradient
    two_new = 0.999 * moment_two + 0.001 * prefix_gradient * prefix_gradient
    one_fix = 1.0 - 0.9 ** STEP
    two_fix = 1.0 - 0.999 ** STEP
    updated = current - 0.02 * (one_new / one_fix) / (jnp.sqrt(two_new / two_fix) + 1e-08)
    return (updated, one_new, two_new)

def one_conversation(states, length, upstream_unshaped, cartridge_keys, cartridge_values, query_weight, key_value_weight, norm_gain):
    sequence_rows = states.shape[0]
    query_group_size = QUERY_HEADS // KEY_VALUE_HEADS
    score_scale = HEAD_SIZE ** (-0.5)
    wide = states.astype(jnp.float32)
    normed = (wide * lax.rsqrt(lax.optimization_barrier(jnp.mean(wide * wide, axis=1, keepdims=True)) + 1e-05) * norm_gain).astype(jnp.bfloat16)
    proj_query = jnp.dot(normed, query_weight, preferred_element_type=jnp.float32)
    project_key_value = jnp.dot(normed, key_value_weight, preferred_element_type=jnp.float32)
    query_rows = rotary_heads(proj_query.reshape(sequence_rows, QUERY_HEADS, HEAD_SIZE), PREFIX_TOKENS).astype(jnp.bfloat16)
    sequence_keys = rotary_heads(project_key_value[:, :KEY_VALUE_HEADS * HEAD_SIZE].reshape(sequence_rows, KEY_VALUE_HEADS, HEAD_SIZE), PREFIX_TOKENS).astype(jnp.bfloat16)
    sequence_values = project_key_value[:, KEY_VALUE_HEADS * HEAD_SIZE:].reshape(sequence_rows, KEY_VALUE_HEADS, HEAD_SIZE).astype(jnp.bfloat16)
    grouped_heads = query_rows.reshape(sequence_rows, KEY_VALUE_HEADS, query_group_size, HEAD_SIZE).astype(jnp.float32)
    keys_wide = cartridge_keys.astype(jnp.float32)
    values_wide = cartridge_values.astype(jnp.float32)
    pre_scores = jnp.einsum('shgd,phd->hgsp', grouped_heads, keys_wide) * score_scale
    own_scores = jnp.einsum('shgd,thd->hgst', grouped_heads, sequence_keys.astype(jnp.float32)) * score_scale
    causal = jnp.arange(sequence_rows)[:, None] >= jnp.arange(sequence_rows)[None, :]
    own_scores = jnp.where(causal, own_scores, -jnp.inf)
    joined = jnp.concatenate([pre_scores, own_scores], axis=-1)
    probs = jax.nn.softmax(joined, axis=-1)
    pre_probs = probs[..., :PREFIX_TOKENS]
    probs_low = probs.astype(jnp.bfloat16).astype(jnp.float32)
    pre_low = probs_low[..., :PREFIX_TOKENS]
    own_low = probs_low[..., PREFIX_TOKENS:]
    attended = jnp.einsum('hgsp,phd->shgd', pre_low, values_wide) + jnp.einsum('hgst,thd->shgd', own_low, sequence_values.astype(jnp.float32))
    active_rows = (jnp.arange(sequence_rows) < length)[:, None, None, None]
    attention_out = jnp.where(active_rows, attended, 0.0).astype(jnp.bfloat16)
    upstream_gradient = jnp.where(active_rows, upstream_unshaped.reshape(sequence_rows, KEY_VALUE_HEADS, query_group_size, HEAD_SIZE), 0.0).astype(jnp.bfloat16)
    upstream_wide = upstream_gradient.astype(jnp.float32)
    delta = jnp.einsum('shgd,shgd->hgs', upstream_wide, attention_out.astype(jnp.float32))
    dprob = jnp.einsum('shgd,phd->hgsp', upstream_wide, values_wide)
    dscore = (pre_probs * (dprob - delta[..., None])).astype(jnp.bfloat16).astype(jnp.float32)
    gradient_keys = jnp.einsum('hgsp,shgd->phd', dscore, grouped_heads) * score_scale
    gradient_values = jnp.einsum('hgsp,shgd->phd', pre_low, upstream_wide)
    conversation_term = jnp.concatenate([gradient_keys.reshape(PREFIX_TOKENS, KEY_VALUE_HEADS * HEAD_SIZE), gradient_values.reshape(PREFIX_TOKENS, KEY_VALUE_HEADS * HEAD_SIZE)], axis=1)
    return (attention_out.reshape(sequence_rows, QUERY_HEADS * HEAD_SIZE), conversation_term)

def reference(hidden, norm_gain, query_weight, key_value_weight, lengths, cotangent, cartridge, adam_first_moment, adam_second_moment):
    cartridge_prefix = cartridge.astype(jnp.bfloat16)
    cartridge_keys = cartridge_prefix[:, :KEY_VALUE_HEADS * HEAD_SIZE].reshape(PREFIX_TOKENS, KEY_VALUE_HEADS, HEAD_SIZE)
    cartridge_values = cartridge_prefix[:, KEY_VALUE_HEADS * HEAD_SIZE:].reshape(PREFIX_TOKENS, KEY_VALUE_HEADS, HEAD_SIZE)

    def accumulate_rows(running, inputs):
        states, length, upstream_unshaped = inputs
        attended, conversation_term = one_conversation(states, length, upstream_unshaped, cartridge_keys, cartridge_values, query_weight, key_value_weight, norm_gain)
        return (running + conversation_term, attended)
    prefix_gradient, layer_outputs = lax.scan(accumulate_rows, jnp.zeros((PREFIX_TOKENS, 2 * KEY_VALUE_HEADS * HEAD_SIZE), jnp.float32), (hidden, lengths, cotangent))
    new_cartridge, new_first, new_second = adam_update(cartridge, adam_first_moment, adam_second_moment, prefix_gradient)
    return (layer_outputs, new_cartridge, new_first, new_second)
```

```python
import functools

import jax
import jax.numpy as jnp
from jax import lax
from jax.experimental import pallas as pl
from jax.experimental.pallas import tpu as pltpu
from jax.sharding import PartitionSpec as P

HEAD_SIZE = 128
QUERY_HEADS = 16
KEY_VALUE_HEADS = 4
GROUP = QUERY_HEADS // KEY_VALUE_HEADS
STEP = 50
LOG2E = 1.4426950408889634


def angle_tables(sequence_rows, offset):
    half_size = HEAD_SIZE // 2
    exponent = jnp.arange(half_size, dtype=jnp.float32) * (2.0 / HEAD_SIZE)
    inverse = jnp.power(jnp.float32(500000.0), -exponent)
    position = (offset + jnp.arange(sequence_rows)).astype(jnp.float32)
    angles = position[:, None] * inverse[None, :]
    cosine, sine = jnp.cos(angles), jnp.sin(angles)
    return (
        jnp.concatenate([cosine, cosine], axis=1),
        jnp.concatenate([-sine, sine], axis=1),
    )


def adam_update(current, moment_one, moment_two, prefix_gradient):
    one_new = 0.9 * moment_one + 0.1 * prefix_gradient
    two_new = 0.999 * moment_two + 0.001 * prefix_gradient * prefix_gradient
    one_fix = 1.0 - 0.9**STEP
    two_fix = 1.0 - 0.999**STEP
    updated = current - 0.02 * (one_new / one_fix) / (jnp.sqrt(two_new / two_fix) + 1e-08)
    return (updated, one_new, two_new)


def dot_f32(left, right, left_dim, right_dim):
    return lax.dot_general(
        left, right, (((left_dim,), (right_dim,)), ((), ())), preferred_element_type=jnp.float32
    )


def attention_kernel(
    length_ref, cos_ref, sin_ref, pq_ref, pk_ref, pv_ref, keys_ref, values_ref, cot_ref,
    out_ref, gk_ref, gv_ref,
):
    rows = pq_ref.shape[0]
    prefix_length = keys_ref.shape[0]
    scale = HEAD_SIZE ** (-0.5)
    cos, sin = cos_ref[...], sin_ref[...]

    def rope(v):
        return (v * cos + pltpu.roll(v, HEAD_SIZE // 2, 1) * sin).astype(jnp.bfloat16)

    length = length_ref[0]
    own_keys = rope(pk_ref[...])
    own_values = pv_ref[...].astype(jnp.bfloat16)
    keys, values = keys_ref[...], values_ref[...]
    causal = lax.broadcasted_iota(jnp.int32, (rows, rows), 0) <= lax.broadcasted_iota(
        jnp.int32, (rows, rows), 1
    )
    active = lax.broadcasted_iota(jnp.int32, (rows, HEAD_SIZE), 0) < length
    active_t = lax.broadcasted_iota(jnp.int32, (HEAD_SIZE, rows), 1) < length
    grad_keys = jnp.zeros((prefix_length, HEAD_SIZE), jnp.float32)
    grad_values = jnp.zeros((prefix_length, HEAD_SIZE), jnp.float32)
    for g in range(GROUP):
        columns = slice(g * HEAD_SIZE, (g + 1) * HEAD_SIZE)
        query = rope(pq_ref[:, columns])
        upstream = jnp.where(active, cot_ref[:, columns].astype(jnp.float32), 0.0)
        upstream_t = upstream.T
        upstream = upstream.astype(jnp.bfloat16)
        pre = dot_f32(keys, query, 1, 1)
        own = jnp.where(causal, dot_f32(own_keys, query, 1, 1), -jnp.inf)
        highest = jnp.maximum(
            jnp.max(pre, axis=0, keepdims=True), jnp.max(own, axis=0, keepdims=True)
        )
        pre = jnp.exp2((pre - highest) * (scale * LOG2E))
        own = jnp.exp2((own - highest) * (scale * LOG2E))
        inverse = 1.0 / (
            jnp.sum(pre, axis=0, keepdims=True) + jnp.sum(own, axis=0, keepdims=True)
        )
        pre = pre * inverse
        pre_low = pre.astype(jnp.bfloat16)
        own_low = (own * inverse).astype(jnp.bfloat16)
        attended = dot_f32(values, pre_low, 0, 0) + dot_f32(own_values, own_low, 0, 0)
        attended = jnp.where(active_t, attended, 0.0).astype(jnp.bfloat16).astype(jnp.float32)
        delta = jnp.sum(upstream_t * attended, axis=0, keepdims=True)
        out_ref[:, columns] = attended.T.astype(jnp.bfloat16)
        dprob = dot_f32(values, upstream, 1, 1)
        dscore = (pre * (dprob - delta)).astype(jnp.bfloat16)
        grad_keys = grad_keys + dot_f32(dscore, query, 1, 0)
        grad_values = grad_values + dot_f32(pre_low, upstream, 1, 0)
    gk_ref[...] = (grad_keys * scale).astype(gk_ref.dtype)
    gv_ref[...] = grad_values.astype(gv_ref.dtype)


def attention(lengths, cos, sin, pq, pkv, prefix, cot, grad_dtype):
    rows, prefix_length = pq.shape[0], prefix.shape[0]
    d, kv = HEAD_SIZE, KEY_VALUE_HEADS
    full = pl.BlockSpec((rows, d), lambda h: (0, 0))
    key_block = lambda n: pl.BlockSpec((n, d), lambda h: (0, h))
    value_block = lambda n: pl.BlockSpec((n, d), lambda h: (0, h + kv))
    wide = pl.BlockSpec((rows, GROUP * d), lambda h: (0, h))
    grad = jax.ShapeDtypeStruct((prefix_length, kv * d), grad_dtype)
    return pl.pallas_call(
        attention_kernel,
        grid=(kv,),
        in_specs=[
            pl.BlockSpec(memory_space=pltpu.SMEM), full, full, wide,
            key_block(rows), value_block(rows),
            key_block(prefix_length), value_block(prefix_length), wide,
        ],
        out_specs=(wide, key_block(prefix_length), key_block(prefix_length)),
        out_shape=(jax.ShapeDtypeStruct((rows, QUERY_HEADS * d), jnp.bfloat16), grad, grad),
        compiler_params=pltpu.CompilerParams(vmem_limit_bytes=32 * 1024 * 1024),
        cost_estimate=pl.CostEstimate(
            flops=2 * QUERY_HEADS * rows * d * (5 * prefix_length + 2 * rows),
            bytes_accessed=10 * 1024 * 1024,
            transcendentals=QUERY_HEADS * rows * (prefix_length + rows),
        ),
        name="attention",
    )(lengths, cos, sin, pq, pkv, pkv, prefix, prefix, cot)


def add_rows(pieces, features):
    return (
        jnp.dot(features, pieces[0], preferred_element_type=jnp.float32),
        jnp.dot(features, pieces[1], preferred_element_type=jnp.float32),
    )


def on_device(
    hidden,
    norm_gain,
    query_weight,
    key_value_weight,
    lengths,
    cotangent,
    cartridge,
    adam_first_moment,
    adam_second_moment,
):
    sequence_rows = hidden.shape[1]
    states = hidden[0].astype(jnp.float32)
    normed = (
        states * lax.rsqrt(jnp.mean(states * states, axis=1, keepdims=True) + 1e-05) * norm_gain
    ).astype(jnp.bfloat16)
    exchanged = lax.all_to_all(normed[None], "fsdp", split_axis=2, concat_axis=0, tiled=True)
    pair_rows = exchanged.reshape(-1, exchanged.shape[2])
    part_query, part_keyval = add_rows(
        (
            lax.all_gather(query_weight, "dp", axis=0, tiled=True),
            lax.all_gather(key_value_weight, "dp", axis=0, tiled=True),
        ),
        pair_rows,
    )
    proj_query, project_key_value = (
        lax.psum_scatter(part_query, "fsdp", scatter_dimension=0, tiled=True),
        lax.psum_scatter(part_keyval, "fsdp", scatter_dimension=0, tiled=True),
    )
    shard_rows = cartridge.shape[0]
    prefix_length = shard_rows * lax.axis_size("owner")
    gathered_rows = lax.all_gather(cartridge.astype(jnp.bfloat16), "owner", axis=0, tiled=True)
    cos, sin = angle_tables(sequence_rows, prefix_length)
    attention_out, gradient_keys, gradient_values = attention(
        lengths, cos, sin, proj_query, project_key_value, gathered_rows, cotangent[0],
        jnp.float32,
    )
    prefix_gradient = jnp.concatenate([gradient_keys, gradient_values], axis=1)
    summed = lax.psum(prefix_gradient, ("fsdp", "dp", "owner"))
    owned_sum = lax.dynamic_slice_in_dim(
        summed, lax.axis_index("owner") * shard_rows, shard_rows, 0
    )
    new_cartridge, new_first, new_second = adam_update(
        cartridge, adam_first_moment, adam_second_moment, owned_sum
    )
    return (
        attention_out.reshape(1, sequence_rows, QUERY_HEADS * HEAD_SIZE),
        new_cartridge,
        new_first,
        new_second,
    )


def solution(mesh):
    placed = (
        P(("fsdp", "dp", "owner"), None, None),
        P(),
        P(("fsdp", "dp"), None),
        P(("fsdp", "dp"), None),
        P(("fsdp", "dp", "owner")),
        P(("fsdp", "dp", "owner"), None, None),
        P("owner", None),
        P("owner", None),
        P("owner", None),
    )
    return jax.shard_map(
        on_device,
        mesh=mesh,
        in_specs=placed,
        out_specs=(
            P(("fsdp", "dp", "owner"), None, None),
            P("owner", None),
            P("owner", None),
            P("owner", None),
        ),
        check_vma=False,
    )
```
